32 devices in a mesh: parts: 2 (over x), chan: 16 (over z, y, core).
Axes of the slice: x: 2, y: 2, z: 4, core: 2. Of those that a mesh axis runs over, the one named last changes fastest.
Arguments:
- spectra: bfloat16 [1024, 8, 1024], P(('parts', 'chan')), parts along dimension 0, may hold values from -8 to 8
- source_blocks: int32 [4, 2], P('parts'), parts along dimension 0, may hold values from 0 to 15
- window_valid: int32 [16], P('parts'), parts along dimension 0, may hold values 0 or 1
Outputs:
- correlations: bfloat16 [2, 2, 32, 1024, 512], P(None, None, None, ('parts', 'chan')), parts along dimension 3
The draws below stay inside these ranges and needn't reach their ends.
There are 2 independent parts, one for each index of `parts`. The reference program is written for one: setup_inputs(seed, part) draws one part's arguments, and reference() takes and returns one part's arrays. A program takes and returns all parts, laid end to end along the dimension named above; each array names one. Nothing has to cross between parts.
All inputs are finite; a program needn't handle non-finite values. Where the reference program divides by a largest or mean magnitude, that divisor is 1e-20 or more.
Results may differ from the reference program's by a relative error of at most 0.0045.
Values may be sent and summed in bfloat16 or wider, within the bound.
A program may use at most 192 MiB of HBM per device.

```python
import math
import jax
import jax.numpy as jnp
from jax import lax

SOURCE = 32
F = 512
LAGS = 512
STEPS = 2
CH_DEV = 32
W = 8
C = 512
NBLK = 16


def draw_spectra(key, part):
    key_noise = jax.random.fold_in(key, 11)
    key_shared = jax.random.fold_in(key, 12)
    key_sign = jax.random.fold_in(key, 13)
    key_level = jax.random.fold_in(key, 14)
    key_factor = jax.random.fold_in(key, 15)
    noise = jax.random.normal(key_noise, (C, W, 2 * F), jnp.float32)
    low_level = 0.25
    high_level = 2.5
    low_factor = 0.8
    high_factor = 1.25
    shared = jax.random.normal(key_shared, (1, W, 2 * F), jnp.float32)
    signs = jnp.where(jax.random.bernoulli(key_sign, 0.5, (C, 1, 1)), 1.0, -1.0).astype(jnp.float32)
    log_level = jax.random.uniform(key_level, (NBLK, 1, 1, 1), jnp.float32, math.log(low_level), math.log(high_level))
    factor = jax.random.uniform(key_factor, (NBLK, SOURCE, 1, 1), jnp.float32, low_factor, high_factor)
    amplitude = (jnp.exp(log_level) * factor).reshape(C, 1, 1)
    values = amplitude * 0.7 * (noise + signs * shared)
    return jnp.clip(values, -8.0, 8.0).astype(jnp.bfloat16)


def with_ends(array, stream_key, least, top_value):
    shape = array.shape
    spot = [jax.random.randint(jax.random.fold_in(stream_key, axis), (), 0, shape[axis]) for axis in range(len(shape))]
    array = array.at[tuple(spot)].set(least)
    longest = shape.index(max(shape))
    spot[longest] = (spot[longest] + 1) % shape[longest]
    return array.at[tuple(spot)].set(top_value)


def setup_inputs(seed: int = 0, part: int = 0) -> dict:
    arg_keys = jax.random.split(jax.random.key(seed), 4)
    own_keys = jax.random.split(jax.random.fold_in(arg_keys[3], part), 4)
    return {
        "spectra": draw_spectra(jax.random.fold_in(jax.random.fold_in(arg_keys[3], part), 71), part),
        "source_blocks": with_ends(jax.random.randint(own_keys[1], (STEPS, 2), 0, NBLK), jax.random.fold_in(own_keys[1], 1), 0, NBLK - 1).astype(jnp.int32),
        "window_valid": with_ends((jax.random.randint(own_keys[2], (W,), 0, 4) < 3).astype(jnp.int32), jax.random.fold_in(own_keys[2], 1), 0, 1),
    }


def build_table(bins, lags):
    freq = jnp.arange(bins, dtype=jnp.int32)[:, None]
    shifted = jnp.arange(lags, dtype=jnp.int32)[None, :] - lags // 2
    phase = jnp.remainder(freq * shifted, 2 * bins).astype(jnp.float32)
    theta = phase * (2.0 * math.pi / (2 * bins))
    weight = jnp.where(freq == 0, 1.0, 2.0).astype(jnp.float32) / (2 * bins)
    return jnp.concatenate([weight * jnp.cos(theta), -weight * jnp.sin(theta)], axis=0).astype(jnp.bfloat16)


def reference(spectra, source_blocks, window_valid):
    lag_table = build_table(F, LAGS)
    window_mask = window_valid.astype(jnp.bfloat16)[None, :, None]
    receiver_groups = spectra.reshape(C // CH_DEV, CH_DEV, W, 2 * F)
    results = []
    for step in range(STEPS):
        pair = []
        for slot in range(2):
            block_index = source_blocks[step, slot]
            source = lax.dynamic_slice_in_dim(spectra, (block_index * SOURCE).astype(jnp.int32), SOURCE, 0) * window_mask
            real_src = source[..., :F].astype(jnp.float32)
            imag_src = source[..., F:].astype(jnp.float32)

            def one_group(group):
                real_rcv = group[..., :F].astype(jnp.float32)
                imag_rcv = group[..., F:].astype(jnp.float32)
                real_part = jnp.einsum("swf,rwf->srf", real_src, real_rcv) + jnp.einsum("swf,rwf->srf", imag_src, imag_rcv)
                imag_part = jnp.einsum("swf,rwf->srf", real_src, imag_rcv) - jnp.einsum("swf,rwf->srf", imag_src, real_rcv)
                cross = jnp.concatenate([real_part, imag_part], axis=2).astype(jnp.bfloat16)
                flat = cross.reshape(SOURCE * CH_DEV, 2 * F)
                return jnp.dot(flat, lag_table, preferred_element_type=jnp.float32).reshape(SOURCE, CH_DEV, LAGS)

            traces = lax.map(one_group, receiver_groups)
            peak = jnp.max(jnp.abs(traces), axis=(0, 2, 3))
            normed = (traces / (peak[None, :, None, None] + 1e-6)).astype(jnp.bfloat16)
            pair.append(jnp.transpose(normed, (1, 0, 2, 3)).reshape(SOURCE, C, LAGS))
        results.append(jnp.stack(pair, axis=0))
    return jnp.stack(results, axis=0)
```

```python
import functools
import math

import jax
import jax.numpy as jnp
import ml_dtypes
import numpy as np
from jax import lax
from jax.experimental import pallas as pl
from jax.experimental.pallas import tpu as pltpu
from jax.sharding import PartitionSpec as P

SOURCE = 32
LAGS = 512
GROUP = 16
VMEM_LIMIT = 56 * 1024 * 1024


def build_table(bins, lags):
    freq = np.arange(bins)[:, None]
    shifted = np.arange(lags)[None, :] - lags // 2
    theta = np.remainder(freq * shifted, 2 * bins) * (2.0 * math.pi / (2 * bins))
    weight = np.where(freq == 0, 1.0, 2.0) / (2 * bins)
    table = np.concatenate([weight * np.cos(theta), -weight * np.sin(theta)], axis=0)
    return table.astype(np.float32).astype(ml_dtypes.bfloat16)


def at_chan(index):
    return {"chan": index}


def greet_all(n, me):
    barrier = pltpu.get_barrier_semaphore()
    for off in range(1, n):
        pl.semaphore_signal(
            barrier, inc=1, device_id=at_chan(lax.rem(me + off, n)),
            device_id_type=pl.DeviceIdType.MESH,
        )
    pl.semaphore_wait(barrier, n - 1)


def gather_kernel(n, x_ref, blocks_ref, mask_ref, out_ref, cand, held, a_send, a_recv, g_send, g_recv):
    me = lax.axis_index("chan")
    z = me // 4
    y = lax.rem(me // 2, 2)
    core = lax.rem(me, 2)
    per = x_ref.shape[0] // n
    greet_all(n, me)

    def a_copy(off):
        to = lax.rem(me + off, n)
        return pltpu.make_async_remote_copy(
            src_ref=x_ref.at[pl.ds(to * per, per)], dst_ref=cand.at[me],
            send_sem=a_send.at[off], recv_sem=a_recv.at[me],
            device_id=at_chan(to), device_id_type=pl.DeviceIdType.MESH,
        )

    for off in range(1, n):
        a_copy(off).start()
    cand[me] = x_ref[pl.ds(me * per, per)]
    for off in range(1, n):
        frm = lax.rem(me + n - off, n)
        pltpu.make_async_remote_copy(
            src_ref=cand.at[frm], dst_ref=cand.at[frm],
            send_sem=a_send.at[off], recv_sem=a_recv.at[frm],
            device_id=at_chan(frm), device_id_type=pl.DeviceIdType.MESH,
        ).wait_recv()
    mask = mask_ref[...]
    for k in range(4):
        b = blocks_ref[k // 2, k % 2]
        held[pl.ds(me * per, per), SOURCE * k:SOURCE * (k + 1), :] = cand[b] * mask

    def index(zz, yy, cc):
        return (zz * 2 + yy) * 2 + cc

    def g_copy(piece, to, lane):
        ref = held.at[pl.ds(piece * per, per)]
        return pltpu.make_async_remote_copy(
            src_ref=ref, dst_ref=ref, send_sem=g_send.at[lane, piece],
            recv_sem=g_recv.at[piece], device_id=at_chan(to),
            device_id_type=pl.DeviceIdType.MESH,
        )

    y_mate = index(z, 1 - y, core)
    c_mate = index(z, y, 1 - core)
    up = lax.rem(me + 4, n)
    down = lax.rem(me + n - 4, n)

    sent = []

    def send(cond, copy):
        sent.append((cond, copy))
        if cond is None:
            copy.start()
        else:
            pl.when(cond)(copy.start)

    def arrive(cond, piece):
        copy = g_copy(piece, c_mate, 0)
        if cond is None:
            copy.wait_recv()
        else:
            pl.when(cond)(copy.wait_recv)

    send(z < 3, g_copy(me, up, 0))
    send(z > 0, g_copy(me, down, 1))
    send(None, g_copy(me, y_mate, 2))
    send(None, g_copy(me, c_mate, 3))

    def y_arrived(cond, zz):
        piece = index(zz, 1 - y, core)
        arrive(cond, piece)
        send(cond, g_copy(piece, c_mate, 3))

    def clamp(zz):
        return jnp.clip(zz, 0, 3)

    for d in range(1, 4):
        low, low_z = z >= d, clamp(z - d)
        high, high_z = z + d <= 3, clamp(z + d)
        for cond, zz, onward, to, lane in (
            (low, low_z, jnp.logical_and(low, z < 3), up, 0),
            (high, high_z, jnp.logical_and(high, z > 0), down, 1),
        ):
            piece = index(zz, y, core)
            arrive(cond, piece)
            send(onward, g_copy(piece, to, lane))
            send(cond, g_copy(piece, y_mate, 2))
            send(cond, g_copy(piece, c_mate, 3))
        if d == 1:
            y_arrived(None, z)
        else:
            y_arrived(z >= d - 1, clamp(z - d + 1))
            y_arrived(z + d - 1 <= 3, clamp(z + d - 1))
    y_arrived(z >= 3, clamp(z - 3))
    y_arrived(z <= 0, clamp(z + 3))
    for zz in range(4):
        for yy in range(2):
            arrive(None, index(zz, yy, 1 - core))
    for off in range(1, n):
        a_copy(off).wait_send()
    for cond, copy in sent:
        if cond is None:
            copy.wait_send()
        else:
            pl.when(cond)(copy.wait_send)
    out_ref[...] = held[...]


def gather_sources(n, x, blocks, mask):
    groups, channels, depth = x.shape
    vmem = pl.BlockSpec(memory_space=pltpu.VMEM)
    return pl.pallas_call(
        functools.partial(gather_kernel, n),
        out_shape=jax.ShapeDtypeStruct((groups, 4 * SOURCE, depth), x.dtype),
        in_specs=[vmem, pl.BlockSpec(memory_space=pltpu.SMEM), vmem],
        out_specs=vmem,
        scratch_shapes=[
            pltpu.VMEM((n, groups // n, channels, depth), x.dtype),
            pltpu.VMEM((groups, 4 * SOURCE, depth), x.dtype),
            pltpu.SemaphoreType.DMA((n,)),
            pltpu.SemaphoreType.DMA((n,)),
            pltpu.SemaphoreType.DMA((4, n)),
            pltpu.SemaphoreType.DMA((n,)),
        ],
        compiler_params=pltpu.CompilerParams(
            collective_id=0, has_side_effects=True, vmem_limit_bytes=VMEM_LIMIT
        ),
        name="gather_sources",
    )(x, blocks, mask)


def correlate_kernel(s_ref, x_ref, table_ref, trace_ref, peak_ref, cross, pk):
    groups, rows, depth = s_ref.shape
    receivers = x_ref.shape[1]
    half = depth // 2
    diag = lax.rem(lax.broadcasted_iota(jnp.int32, (GROUP, depth), 1), GROUP) == (
        lax.broadcasted_iota(jnp.int32, (GROUP, depth), 0)
    )

    def first(g, carry):
        v = x_ref[g].astype(jnp.float32)
        turned = jnp.concatenate([v[:, half:], -v[:, :half]], axis=1)
        both = jnp.stack([v, turned], axis=1)
        spread = jnp.where(diag[None, None], both[:, :, None, :], 0.0).astype(jnp.bfloat16)
        spread = spread.reshape(receivers * 2 * GROUP, depth)
        out = lax.dot_general(
            spread, s_ref[g], (((1,), (1,)), ((), ())), preferred_element_type=jnp.float32
        ).astype(jnp.bfloat16)
        where = pl.ds(pl.multiple_of(g * GROUP, GROUP), GROUP)
        cross[:, :, where, :] = out.reshape(receivers, 2, GROUP, rows)
        return carry

    lax.fori_loop(0, groups, first, 0)

    pk[...] = jnp.zeros_like(pk)
    step = 4
    lanes = pk.shape[1]

    def second(i, carry):
        parts = [
            cross[i * step + q].reshape(2 * groups * GROUP, rows).T for q in range(step)
        ]
        out = jnp.dot(
            jnp.concatenate(parts, axis=0), table_ref[...], preferred_element_type=jnp.float32
        )
        best = pk[...]
        for q in range(step):
            piece = out[q * rows:(q + 1) * rows]
            for c in range(LAGS // lanes):
                cols = piece[:, c * lanes:(c + 1) * lanes]
                trace_ref[c, pl.ds(i * step + q, rows, stride=receivers), :] = cols
                best = jnp.maximum(best, jnp.abs(cols))
        pk[...] = best
        return carry

    lax.fori_loop(0, receivers // step, second, 0)
    peak_ref[...] = jnp.broadcast_to(jnp.max(pk[...].T, axis=0, keepdims=True), peak_ref.shape)


def correlate(sources, x, table):
    groups, rows, depth = sources.shape
    receivers = x.shape[1]
    vmem = pl.BlockSpec(memory_space=pltpu.VMEM)
    return pl.pallas_call(
        correlate_kernel,
        out_shape=(
            jax.ShapeDtypeStruct((LAGS // 128, rows * receivers, 128), jnp.float32),
            jax.ShapeDtypeStruct((8, rows), jnp.float32),
        ),
        in_specs=[vmem] * 3,
        out_specs=(vmem, vmem),
        scratch_shapes=[
            pltpu.VMEM((receivers, 2, groups * GROUP, rows), jnp.bfloat16),
            pltpu.VMEM((rows, 128), jnp.float32),
        ],
        compiler_params=pltpu.CompilerParams(vmem_limit_bytes=VMEM_LIMIT),
        name="correlate",
    )(sources, x, table)


def peak_kernel(n, peak_ref, out_ref, slots, send_sem, recv_sem):
    me = lax.axis_index("chan")
    greet_all(n, me)

    def copy(off):
        return pltpu.make_async_remote_copy(
            src_ref=peak_ref, dst_ref=slots.at[me], send_sem=send_sem.at[off],
            recv_sem=recv_sem.at[me], device_id=at_chan(lax.rem(me + off, n)),
            device_id_type=pl.DeviceIdType.MESH,
        )

    for off in range(1, n):
        copy(off).start()
    slots[me] = peak_ref[...]
    for off in range(1, n):
        frm = lax.rem(me + n - off, n)
        pltpu.make_async_remote_copy(
            src_ref=slots.at[frm], dst_ref=slots.at[frm], send_sem=send_sem.at[off],
            recv_sem=recv_sem.at[frm], device_id=at_chan(frm),
            device_id_type=pl.DeviceIdType.MESH,
        ).wait_recv()
    out_ref[...] = jnp.max(slots[...], axis=0)
    for off in range(1, n):
        copy(off).wait_send()


def share_peak(n, peak):
    vmem = pl.BlockSpec(memory_space=pltpu.VMEM)
    return pl.pallas_call(
        functools.partial(peak_kernel, n),
        out_shape=jax.ShapeDtypeStruct(peak.shape, peak.dtype),
        in_specs=[vmem],
        out_specs=vmem,
        scratch_shapes=[
            pltpu.VMEM((n,) + peak.shape, peak.dtype),
            pltpu.SemaphoreType.DMA((n,)),
            pltpu.SemaphoreType.DMA((n,)),
        ],
        compiler_params=pltpu.CompilerParams(collective_id=1, has_side_effects=True),
        name="share_peak",
    )(peak)


def scale_kernel(block, receivers, peak_ref, trace_ref, out_ref):
    i = pl.program_id(0)
    for q in range(block):
        peak = jnp.full((1, 128), peak_ref[0, i * block + q], jnp.float32)
        inverse = 1.0 / (peak + 1e-06)
        here = slice(q * receivers, (q + 1) * receivers)
        for c in range(LAGS // 128):
            cols = slice(c * 128, (c + 1) * 128)
            out_ref[here, cols] = (trace_ref[c, here, :] * inverse).astype(jnp.bfloat16)


def scale(trace, peak, receivers):
    block = 16
    total = trace.shape[1]
    steps = total // (block * receivers)
    return pl.pallas_call(
        functools.partial(scale_kernel, block, receivers),
        out_shape=jax.ShapeDtypeStruct((total, LAGS), jnp.bfloat16),
        grid=(steps,),
        in_specs=[
            pl.BlockSpec(memory_space=pltpu.SMEM),
            pl.BlockSpec((LAGS // 128, block * receivers, 128), lambda i: (0, i, 0)),
        ],
        out_specs=pl.BlockSpec((block * receivers, LAGS), lambda i: (i, 0)),
        compiler_params=pltpu.CompilerParams(vmem_limit_bytes=VMEM_LIMIT),
        name="scale",
    )(peak, trace)


def shards(n, spectra, source_blocks, window_valid):
    receivers, windows, width = spectra.shape
    bins = width // 2
    groups = bins // GROUP
    num_steps = source_blocks.shape[0]
    x = spectra.reshape(receivers, windows, 2, groups, GROUP).transpose(3, 0, 2, 1, 4)
    x = x.reshape(groups, receivers, 2 * windows * GROUP)
    mask = jnp.tile(jnp.repeat(window_valid.astype(jnp.bfloat16), GROUP), 2)[None, :]
    table = jnp.asarray(build_table(bins, LAGS))
    if n == 16:
        sources = gather_sources(n, x, source_blocks, mask)
    else:
        roots = source_blocks.reshape(-1) // (receivers // SOURCE)
        mine = (roots == lax.axis_index("chan"))[None, :, None, None]
        picked = jnp.where(mine, (x * mask)[:, None], jnp.zeros((), x.dtype))
        sources = lax.psum(picked.reshape(groups, -1, x.shape[2]), "chan")
    trace, peak = correlate(sources, x, table)
    peak = share_peak(n, peak) if n == 16 else lax.pmax(peak, "chan")
    out = scale(trace, peak, receivers)
    return out.reshape(num_steps, 2, SOURCE, receivers, LAGS)


def solution(mesh):
    placed = (P(("parts", "chan"), None, None), P("parts", None), P("parts"))
    return jax.shard_map(
        functools.partial(shards, mesh.shape["chan"]),
        mesh=mesh,
        in_specs=placed,
        out_specs=P(None, None, None, ("parts", "chan"), None),
        check_vma=False,
    )
```

```python
import functools
import math

import jax
import jax.numpy as jnp
import ml_dtypes
import numpy as np
from jax import lax
from jax.experimental import pallas as pl
from jax.experimental.pallas import tpu as pltpu
from jax.sharding import PartitionSpec as P

SOURCE = 32
LAGS = 512
GROUP = 16
VMEM_LIMIT = 56 * 1024 * 1024


def build_table(bins, lags):
    freq = np.arange(bins)[:, None]
    shifted = np.arange(lags)[None, :] - lags // 2
    theta = np.remainder(freq * shifted, 2 * bins) * (2.0 * math.pi / (2 * bins))
    weight = np.where(freq == 0, 1.0, 2.0) / (2 * bins)
    table = np.concatenate([weight * np.cos(theta), -weight * np.sin(theta)], axis=0)
    return table.astype(np.float32).astype(ml_dtypes.bfloat16)


def at_chan(index):
    return {"chan": index}


def fused_kernel(
    n, a_ref, blocks_ref, valid_ref, rows_ref, cols_ref, table_ref, out_ref,
    x, cand0, cand1, held, spread, cross, trace, stage, pk, slots, inverse,
    a_send, a_recv, g_send, g_recv, p_send, p_recv, o_sem,
):
    me = lax.axis_index("chan")
    z = me // 4
    y = lax.rem(me // 2, 2)
    core = lax.rem(me, 2)
    groups, receivers, depth = x.shape
    per = groups // n
    half = depth // 2
    rows = held.shape[1]
    mesh_ids = pl.DeviceIdType.MESH
    cand = (cand0, cand1)

    barrier = pltpu.get_barrier_semaphore()
    for off in range(1, n):
        pl.semaphore_signal(
            barrier, inc=1, device_id=at_chan(lax.rem(me + off, n)), device_id_type=mesh_ids
        )

    by_window = jnp.dot(
        rows_ref[...], a_ref[...], preferred_element_type=jnp.float32
    ).astype(jnp.bfloat16)
    windows = by_window.shape[0] // receivers
    tiles = by_window.shape[1] // half
    flat = jnp.concatenate(
        [
            jnp.concatenate(
                [
                    by_window[w * receivers:(w + 1) * receivers, t * half:(t + 1) * half]
                    for w in range(windows)
                ],
                axis=1,
            )
            for t in range(tiles)
        ],
        axis=0,
    )
    turned = jnp.dot(flat, cols_ref[...], preferred_element_type=jnp.float32).astype(jnp.bfloat16)
    high = tiles // 2
    low = groups // high
    for t in range(tiles):
        c, gh = t // high, t % high
        for gl in range(low):
            x[gh * low + gl, :, c * half:(c + 1) * half] = turned[
                t * receivers:(t + 1) * receivers, gl * half:(gl + 1) * half
            ]

    pl.semaphore_wait(barrier, n - 1)

    def a_copy(h, off):
        to = lax.rem(me + off, n)
        return pltpu.make_async_remote_copy(
            src_ref=x.at[to * per + h], dst_ref=cand[h].at[me],
            send_sem=a_send.at[h, off], recv_sem=a_recv.at[h, me],
            device_id=at_chan(to), device_id_type=mesh_ids,
        )

    for h in range(per):
        for off in range(1, n):
            a_copy(h, off).start()
    for h in range(per):
        cand[h][me] = x[me * per + h]

    diag = lax.rem(lax.broadcasted_iota(jnp.int32, (GROUP, depth), 1), GROUP) == (
        lax.broadcasted_iota(jnp.int32, (GROUP, depth), 0)
    )

    def widen(g, carry):
        v = x[g].astype(jnp.float32)
        rotated = jnp.concatenate([v[:, half:], -v[:, :half]], axis=1)
        both = jnp.stack([v, rotated], axis=1)
        wide = jnp.where(diag[None, None], both[:, :, None, :], 0.0).astype(jnp.bfloat16)
        spread[g] = wide.reshape(receivers * 2 * GROUP, depth)
        return carry

    lax.fori_loop(0, groups, widen, 0)

    window = lax.rem(lax.broadcasted_iota(jnp.int32, (1, depth), 1), half) // GROUP
    mask = jnp.zeros((1, depth), jnp.float32)
    for w in range(windows):
        mask = jnp.where(window == w, valid_ref[w].astype(jnp.float32), mask)
    mask = mask.astype(jnp.bfloat16)

    def index(zz, yy, cc):
        return (zz * 2 + yy) * 2 + cc

    def g_copy(h, piece, to, lane):
        ref = held.at[piece * per + h]
        return pltpu.make_async_remote_copy(
            src_ref=ref, dst_ref=ref, send_sem=g_send.at[h, lane, piece],
            recv_sem=g_recv.at[h, piece], device_id=at_chan(to), device_id_type=mesh_ids,
        )

    y_mate = index(z, 1 - y, core)
    c_mate = index(z, y, 1 - core)
    up = lax.rem(me + 4, n)
    down = lax.rem(me + n - 4, n)
    sent = []

    def guarded(cond, action):
        if cond is None:
            action()
        else:
            pl.when(cond)(action)

    def send(cond, copy):
        sent.append((cond, copy))
        guarded(cond, copy.start)

    def arrive(cond, h, piece):
        guarded(cond, g_copy(h, piece, c_mate, 0).wait_recv)

    def first(piece):
        def body(h, carry):
            g = piece * per + h
            out = lax.dot_general(
                spread[g], held[g], (((1,), (1,)), ((), ())), preferred_element_type=jnp.float32
            ).astype(jnp.bfloat16)
            where = pl.ds(pl.multiple_of(g * GROUP, GROUP), GROUP)
            cross[:, :, where, :] = out.reshape(receivers, 2, GROUP, rows)
            return carry

        lax.fori_loop(0, per, body, 0)

    for h in range(per):
        for off in range(1, n):
            frm = lax.rem(me + n - off, n)
            pltpu.make_async_remote_copy(
                src_ref=cand[h].at[frm], dst_ref=cand[h].at[frm],
                send_sem=a_send.at[h, off], recv_sem=a_recv.at[h, frm],
                device_id=at_chan(frm), device_id_type=mesh_ids,
            ).wait_recv()
        for k in range(4):
            b = blocks_ref[k // 2, k % 2]
            held[me * per + h, SOURCE * k:SOURCE * (k + 1), :] = cand[h][b] * mask
        send(z < 3, g_copy(h, me, up, 0))
        send(z > 0, g_copy(h, me, down, 1))
        send(None, g_copy(h, me, y_mate, 2))
        send(None, g_copy(h, me, c_mate, 3))

    def clamp(zz):
        return jnp.clip(zz, 0, 3)

    ready = [(None, me)]

    def y_arrived(cond, zz):
        piece = index(zz, 1 - y, core)
        for h in range(per):
            arrive(cond, h, piece)
            send(cond, g_copy(h, piece, c_mate, 3))
        ready.append((cond, piece))

    def work():
        for cond, piece in ready:
            guarded(cond, functools.partial(first, piece))
        ready.clear()

    for d in range(1, 4):
        low_in, low_z = z >= d, clamp(z - d)
        high_in, high_z = z + d <= 3, clamp(z + d)
        ways = (
            (low_in, low_z, jnp.logical_and(low_in, z < 3), up, 0),
            (high_in, high_z, jnp.logical_and(high_in, z > 0), down, 1),
        )
        for h in range(per):
            for cond, zz, onward, to, lane in ways:
                piece = index(zz, y, core)
                arrive(cond, h, piece)
                send(onward, g_copy(h, piece, to, lane))
                send(cond, g_copy(h, piece, y_mate, 2))
                send(cond, g_copy(h, piece, c_mate, 3))
        if d == 1:
            y_arrived(None, z)
        else:
            y_arrived(z >= d - 1, clamp(z - d + 1))
            y_arrived(z + d - 1 <= 3, clamp(z + d - 1))
        work()
        for cond, zz, _, _, _ in ways:
            ready.append((cond, index(zz, y, core)))
    y_arrived(z >= 3, clamp(z - 3))
    y_arrived(z <= 0, clamp(z + 3))
    work()

    def others(i, carry):
        piece = index(i // 2, lax.rem(i, 2), 1 - core)
        for h in range(per):
            arrive(None, h, piece)
        first(piece)
        return carry

    lax.fori_loop(0, n // 2, others, 0)

    pk[...] = jnp.zeros_like(pk)
    step = 4
    lanes = pk.shape[1]

    def second(i, carry):
        parts = [cross[i * step + q].reshape(2 * groups * GROUP, rows).T for q in range(step)]
        out = jnp.dot(
            jnp.concatenate(parts, axis=0), table_ref[...], preferred_element_type=jnp.float32
        )
        best = pk[...]
        for q in range(step):
            piece = out[q * rows:(q + 1) * rows]
            for c in range(LAGS // lanes):
                part = piece[:, c * lanes:(c + 1) * lanes]
                trace[c, pl.ds(i * step + q, rows, stride=receivers), :] = part
                best = jnp.maximum(best, jnp.abs(part))
        pk[...] = best
        return carry

    lax.fori_loop(0, receivers // step, second, 0)

    own = jnp.max(pk[...].T, axis=0, keepdims=True)
    slots[me] = jnp.broadcast_to(own, slots.shape[1:])

    def p_copy(off):
        return pltpu.make_async_remote_copy(
            src_ref=slots.at[me], dst_ref=slots.at[me], send_sem=p_send.at[off],
            recv_sem=p_recv.at[me], device_id=at_chan(lax.rem(me + off, n)),
            device_id_type=mesh_ids,
        )

    for off in range(1, n):
        p_copy(off).start()
    for h in range(per):
        for off in range(1, n):
            a_copy(h, off).wait_send()
    for cond, copy in sent:
        guarded(cond, copy.wait_send)
    for off in range(1, n):
        frm = lax.rem(me + n - off, n)
        pltpu.make_async_remote_copy(
            src_ref=slots.at[frm], dst_ref=slots.at[frm], send_sem=p_send.at[off],
            recv_sem=p_recv.at[frm], device_id=at_chan(frm), device_id_type=mesh_ids,
        ).wait_recv()
    top = jnp.max(jnp.max(slots[...], axis=0), axis=0, keepdims=True)
    inverse[...] = 1.0 / (jnp.broadcast_to(top, inverse.shape).T + 1e-06)

    block = rows // o_sem.shape[0]
    size = block * receivers

    def o_copy(i):
        here = pl.ds(pl.multiple_of(i * size, size), size)
        return pltpu.make_async_copy(stage.at[here], out_ref.at[here], o_sem.at[i])

    def finish(i, carry):
        for q in range(block):
            row = i * block + q
            factor = inverse[pl.ds(row, 1), :]
            here = pl.ds(pl.multiple_of(row * receivers, receivers), receivers)
            for c in range(LAGS // lanes):
                stage[here, c * lanes:(c + 1) * lanes] = (trace[c, here, :] * factor).astype(
                    jnp.bfloat16
                )
        o_copy(i).start()
        return carry

    lax.fori_loop(0, o_sem.shape[0], finish, 0)
    for off in range(1, n):
        p_copy(off).wait_send()
    for i in range(o_sem.shape[0]):
        o_copy(i).wait()


def reorder_tables(receivers, windows, groups):
    ch, w = np.meshgrid(np.arange(receivers), np.arange(windows), indexing="ij")
    rows = np.zeros((receivers * windows,) * 2, np.float32)
    rows[(w * receivers + ch).ravel(), (ch * windows + w).ravel()] = 1.0
    low = 128 // GROUP
    w, g, f = np.meshgrid(np.arange(windows), np.arange(low), np.arange(GROUP), indexing="ij")
    cols = np.zeros((windows * 128,) * 2, np.float32)
    cols[(w * 128 + g * GROUP + f).ravel(), (g * 128 + w * GROUP + f).ravel()] = 1.0
    return rows.astype(ml_dtypes.bfloat16), cols.astype(ml_dtypes.bfloat16)


def fused(n, spectra, blocks, valid, table):
    receivers, windows, width = spectra.shape
    groups = width // 2 // GROUP
    depth = 2 * windows * GROUP
    sources = 4 * SOURCE
    chunks = 8
    per = groups // n
    vmem = pl.BlockSpec(memory_space=pltpu.VMEM)
    smem = pl.BlockSpec(memory_space=pltpu.SMEM)
    by_row, by_col = reorder_tables(receivers, windows, groups)
    dma = pltpu.SemaphoreType.DMA
    return pl.pallas_call(
        functools.partial(fused_kernel, n),
        out_shape=jax.ShapeDtypeStruct((sources * receivers, LAGS), jnp.bfloat16),
        in_specs=[vmem, smem, smem, vmem, vmem, vmem],
        out_specs=pl.BlockSpec(memory_space=pl.ANY),
        scratch_shapes=[
            pltpu.VMEM((groups, receivers, depth), jnp.bfloat16),
            pltpu.VMEM((n, receivers, depth), jnp.bfloat16),
            pltpu.VMEM((n, receivers, depth), jnp.bfloat16),
            pltpu.VMEM((groups, sources, depth), jnp.bfloat16),
            pltpu.VMEM((groups, receivers * 2 * GROUP, depth), jnp.bfloat16),
            pltpu.VMEM((receivers, 2, groups * GROUP, sources), jnp.bfloat16),
            pltpu.VMEM((LAGS // 128, sources * receivers, 128), jnp.float32),
            pltpu.VMEM((sources * receivers, LAGS), jnp.bfloat16),
            pltpu.VMEM((sources, 128), jnp.float32),
            pltpu.VMEM((n, 8, sources), jnp.float32),
            pltpu.VMEM((sources, 128), jnp.float32),
            dma((per, n)),
            dma((per, n)),
            dma((per, 4, n)),
            dma((per, n)),
            dma((n,)),
            dma((n,)),
            dma((chunks,)),
        ],
        compiler_params=pltpu.CompilerParams(
            collective_id=0, has_side_effects=True, vmem_limit_bytes=VMEM_LIMIT
        ),
        name="fused",
    )(
        spectra.reshape(receivers * windows, width), blocks, valid,
        jnp.asarray(by_row), jnp.asarray(by_col), table,
    )


def correlate_kernel(s_ref, x_ref, table_ref, trace_ref, peak_ref, cross, pk):
    groups, rows, depth = s_ref.shape
    receivers = x_ref.shape[1]
    half = depth // 2
    diag = lax.rem(lax.broadcasted_iota(jnp.int32, (GROUP, depth), 1), GROUP) == (
        lax.broadcasted_iota(jnp.int32, (GROUP, depth), 0)
    )

    def first(g, carry):
        v = x_ref[g].astype(jnp.float32)
        turned = jnp.concatenate([v[:, half:], -v[:, :half]], axis=1)
        both = jnp.stack([v, turned], axis=1)
        spread = jnp.where(diag[None, None], both[:, :, None, :], 0.0).astype(jnp.bfloat16)
        spread = spread.reshape(receivers * 2 * GROUP, depth)
        out = lax.dot_general(
            spread, s_ref[g], (((1,), (1,)), ((), ())), preferred_element_type=jnp.float32
        ).astype(jnp.bfloat16)
        where = pl.ds(pl.multiple_of(g * GROUP, GROUP), GROUP)
        cross[:, :, where, :] = out.reshape(receivers, 2, GROUP, rows)
        return carry

    lax.fori_loop(0, groups, first, 0)

    pk[...] = jnp.zeros_like(pk)
    step = 4
    lanes = pk.shape[1]

    def second(i, carry):
        parts = [
            cross[i * step + q].reshape(2 * groups * GROUP, rows).T for q in range(step)
        ]
        out = jnp.dot(
            jnp.concatenate(parts, axis=0), table_ref[...], preferred_element_type=jnp.float32
        )
        best = pk[...]
        for q in range(step):
            piece = out[q * rows:(q + 1) * rows]
            for c in range(LAGS // lanes):
                cols = piece[:, c * lanes:(c + 1) * lanes]
                trace_ref[c, pl.ds(i * step + q, rows, stride=receivers), :] = cols
                best = jnp.maximum(best, jnp.abs(cols))
        pk[...] = best
        return carry

    lax.fori_loop(0, receivers // step, second, 0)
    peak_ref[...] = jnp.broadcast_to(jnp.max(pk[...].T, axis=0, keepdims=True), peak_ref.shape)


def correlate(sources, x, table):
    groups, rows, depth = sources.shape
    receivers = x.shape[1]
    vmem = pl.BlockSpec(memory_space=pltpu.VMEM)
    return pl.pallas_call(
        correlate_kernel,
        out_shape=(
            jax.ShapeDtypeStruct((LAGS // 128, rows * receivers, 128), jnp.float32),
            jax.ShapeDtypeStruct((8, rows), jnp.float32),
        ),
        in_specs=[vmem] * 3,
        out_specs=(vmem, vmem),
        scratch_shapes=[
            pltpu.VMEM((receivers, 2, groups * GROUP, rows), jnp.bfloat16),
            pltpu.VMEM((rows, 128), jnp.float32),
        ],
        compiler_params=pltpu.CompilerParams(vmem_limit_bytes=VMEM_LIMIT),
        name="correlate",
    )(sources, x, table)


def scale_kernel(block, receivers, peak_ref, trace_ref, out_ref):
    i = pl.program_id(0)
    for q in range(block):
        peak = jnp.full((1, 128), peak_ref[0, i * block + q], jnp.float32)
        inverse = 1.0 / (peak + 1e-06)
        here = slice(q * receivers, (q + 1) * receivers)
        for c in range(LAGS // 128):
            cols = slice(c * 128, (c + 1) * 128)
            out_ref[here, cols] = (trace_ref[c, here, :] * inverse).astype(jnp.bfloat16)


def scale(trace, peak, receivers):
    block = 16
    total = trace.shape[1]
    steps = total // (block * receivers)
    return pl.pallas_call(
        functools.partial(scale_kernel, block, receivers),
        out_shape=jax.ShapeDtypeStruct((total, LAGS), jnp.bfloat16),
        grid=(steps,),
        in_specs=[
            pl.BlockSpec(memory_space=pltpu.SMEM),
            pl.BlockSpec((LAGS // 128, block * receivers, 128), lambda i: (0, i, 0)),
        ],
        out_specs=pl.BlockSpec((block * receivers, LAGS), lambda i: (i, 0)),
        compiler_params=pltpu.CompilerParams(vmem_limit_bytes=VMEM_LIMIT),
        name="scale",
    )(peak, trace)


def shards(n, spectra, source_blocks, window_valid):
    receivers, windows, width = spectra.shape
    bins = width // 2
    groups = bins // GROUP
    num_steps = source_blocks.shape[0]
    table = jnp.asarray(build_table(bins, LAGS))
    if n == 16:
        out = fused(n, spectra, source_blocks, window_valid, table)
    else:
        x = spectra.reshape(receivers, windows, 2, groups, GROUP).transpose(3, 0, 2, 1, 4)
        x = x.reshape(groups, receivers, 2 * windows * GROUP)
        mask = jnp.tile(jnp.repeat(window_valid.astype(jnp.bfloat16), GROUP), 2)[None, :]
        roots = source_blocks.reshape(-1) // (receivers // SOURCE)
        mine = (roots == lax.axis_index("chan"))[None, :, None, None]
        picked = jnp.where(mine, (x * mask)[:, None], jnp.zeros((), x.dtype))
        sources = lax.psum(picked.reshape(groups, -1, x.shape[2]), "chan")
        trace, peak = correlate(sources, x, table)
        out = scale(trace, lax.pmax(peak, "chan"), receivers)
    return out.reshape(num_steps, 2, SOURCE, receivers, LAGS)


def solution(mesh):
    placed = (P(("parts", "chan"), None, None), P("parts", None), P("parts"))
    return jax.shard_map(
        functools.partial(shards, mesh.shape["chan"]),
        mesh=mesh,
        in_specs=placed,
        out_specs=P(None, None, None, ("parts", "chan"), None),
        check_vma=False,
    )
```

```python
import functools
import math

import jax
import jax.numpy as jnp
import ml_dtypes
import numpy as np
from jax import lax
from jax.experimental import pallas as pl
from jax.experimental.pallas import tpu as pltpu
from jax.sharding import PartitionSpec as P

SOURCE = 32
LAGS = 512
GROUP = 16
VMEM_LIMIT = 56 * 1024 * 1024


def build_table(bins, lags):
    freq = np.arange(bins)[:, None]
    shifted = np.arange(lags)[None, :] - lags // 2
    theta = np.remainder(freq * shifted, 2 * bins) * (2.0 * math.pi / (2 * bins))
    weight = np.where(freq == 0, 1.0, 2.0) / (2 * bins)
    table = np.concatenate([weight * np.cos(theta), -weight * np.sin(theta)], axis=0)
    return table.astype(np.float32).astype(ml_dtypes.bfloat16)


def at_chan(index):
    return {"chan": index}


def fused_kernel(
    n, a_ref, blocks_ref, valid_ref, rows_ref, table_hbm, out_ref,
    table_ref, x, cand0, cand1, held, spread, cross, trace, stage, pk, slots, inverse,
    a_send, a_recv, g_send, g_recv, p_send, p_recv, o_sem, t_sem,
):
    me = lax.axis_index("chan")
    z = me // 4
    y = lax.rem(me // 2, 2)
    core = lax.rem(me, 2)
    groups, receivers, depth = x.shape
    per = groups // n
    half = depth // 2
    rows = held.shape[1]
    mesh_ids = pl.DeviceIdType.MESH
    cand = (cand0, cand1)

    table_copy = pltpu.make_async_copy(table_hbm, table_ref, t_sem)
    table_copy.start()
    barrier = pltpu.get_barrier_semaphore()
    for off in range(1, n):
        pl.semaphore_signal(
            barrier, inc=1, device_id=at_chan(lax.rem(me + off, n)), device_id_type=mesh_ids
        )

    low = half // GROUP
    row = lax.broadcasted_iota(jnp.int32, (depth * 4, half), 0)
    lane = lax.broadcasted_iota(jnp.int32, (depth * 4, half), 1)
    target = (row // half) * GROUP + lax.rem(row, GROUP)
    here = lane == target
    belongs = lax.rem(row, half) // GROUP
    cols = jnp.concatenate(
        [
            jnp.where(jnp.logical_and(here, belongs == t), 1.0, 0.0).astype(jnp.bfloat16)
            for t in range(low)
        ],
        axis=1,
    )

    by_window = jnp.dot(
        rows_ref[...], a_ref[...], preferred_element_type=jnp.float32
    ).astype(jnp.bfloat16)
    windows = by_window.shape[0] // receivers
    tiles = by_window.shape[1] // half
    flat = jnp.concatenate(
        [
            jnp.concatenate(
                [
                    by_window[w * receivers:(w + 1) * receivers, t * half:(t + 1) * half]
                    for w in range(windows)
                ],
                axis=1,
            )
            for t in range(tiles)
        ],
        axis=0,
    )
    turned = jnp.dot(flat, cols, preferred_element_type=jnp.float32).astype(jnp.bfloat16)
    high = tiles // 2
    for t in range(tiles):
        c, gh = t // high, t % high
        for gl in range(low):
            x[gh * low + gl, :, c * half:(c + 1) * half] = turned[
                t * receivers:(t + 1) * receivers, gl * half:(gl + 1) * half
            ]

    pl.semaphore_wait(barrier, n - 1)

    def a_copy(h, off):
        to = lax.rem(me + off, n)
        return pltpu.make_async_remote_copy(
            src_ref=x.at[to * per + h], dst_ref=cand[h].at[me],
            send_sem=a_send.at[h, off], recv_sem=a_recv.at[h, me],
            device_id=at_chan(to), device_id_type=mesh_ids,
        )

    for h in range(per):
        for off in range(1, n):
            a_copy(h, off).start()
    for h in range(per):
        cand[h][me] = x[me * per + h]

    diag = lax.rem(lax.broadcasted_iota(jnp.int32, (GROUP, depth), 1), GROUP) == (
        lax.broadcasted_iota(jnp.int32, (GROUP, depth), 0)
    )

    def widen(g, carry):
        v = x[g].astype(jnp.float32)
        rotated = jnp.concatenate([v[:, half:], -v[:, :half]], axis=1)
        both = jnp.stack([v, rotated], axis=1)
        wide = jnp.where(diag[None, None], both[:, :, None, :], 0.0).astype(jnp.bfloat16)
        spread[g] = wide.reshape(receivers * 2 * GROUP, depth)
        return carry

    lax.fori_loop(0, groups, widen, 0)

    window = lax.rem(lax.broadcasted_iota(jnp.int32, (1, depth), 1), half) // GROUP
    mask = jnp.zeros((1, depth), jnp.float32)
    for w in range(windows):
        mask = jnp.where(window == w, valid_ref[w].astype(jnp.float32), mask)
    mask = mask.astype(jnp.bfloat16)

    def index(zz, yy, cc):
        return (zz * 2 + yy) * 2 + cc

    def g_copy(h, piece, to, lane):
        ref = held.at[piece * per + h]
        return pltpu.make_async_remote_copy(
            src_ref=ref, dst_ref=ref, send_sem=g_send.at[h, lane, piece],
            recv_sem=g_recv.at[h, piece], device_id=at_chan(to), device_id_type=mesh_ids,
        )

    y_mate = index(z, 1 - y, core)
    c_mate = index(z, y, 1 - core)
    up = lax.rem(me + 4, n)
    down = lax.rem(me + n - 4, n)
    sent = []

    def guarded(cond, action):
        if cond is None:
            action()
        else:
            pl.when(cond)(action)

    def send(cond, copy):
        sent.append((cond, copy))
        guarded(cond, copy.start)

    def arrive(cond, h, piece):
        guarded(cond, g_copy(h, piece, c_mate, 0).wait_recv)

    def first(piece):
        def body(h, carry):
            g = piece * per + h
            out = lax.dot_general(
                spread[g], held[g], (((1,), (1,)), ((), ())), preferred_element_type=jnp.float32
            ).astype(jnp.bfloat16)
            where = pl.ds(pl.multiple_of(g * GROUP, GROUP), GROUP)
            cross[:, :, where, :] = out.reshape(receivers, 2, GROUP, rows)
            return carry

        lax.fori_loop(0, per, body, 0)

    for h in range(per):
        for off in range(1, n):
            frm = lax.rem(me + n - off, n)
            pltpu.make_async_remote_copy(
                src_ref=cand[h].at[frm], dst_ref=cand[h].at[frm],
                send_sem=a_send.at[h, off], recv_sem=a_recv.at[h, frm],
                device_id=at_chan(frm), device_id_type=mesh_ids,
            ).wait_recv()
        for k in range(4):
            b = blocks_ref[k // 2, k % 2]
            held[me * per + h, SOURCE * k:SOURCE * (k + 1), :] = cand[h][b] * mask
        send(z < 3, g_copy(h, me, up, 0))
        send(z > 0, g_copy(h, me, down, 1))
        send(None, g_copy(h, me, y_mate, 2))
        send(None, g_copy(h, me, c_mate, 3))

    def clamp(zz):
        return jnp.clip(zz, 0, 3)

    ready = [(None, me)]

    def y_arrived(cond, zz):
        piece = index(zz, 1 - y, core)
        for h in range(per):
            arrive(cond, h, piece)
            send(cond, g_copy(h, piece, c_mate, 3))
        ready.append((cond, piece))

    def work():
        for cond, piece in ready:
            guarded(cond, functools.partial(first, piece))
        ready.clear()

    for d in range(1, 4):
        low_in, low_z = z >= d, clamp(z - d)
        high_in, high_z = z + d <= 3, clamp(z + d)
        ways = (
            (low_in, low_z, jnp.logical_and(low_in, z < 3), up, 0),
            (high_in, high_z, jnp.logical_and(high_in, z > 0), down, 1),
        )
        for h in range(per):
            for cond, zz, onward, to, lane in ways:
                piece = index(zz, y, core)
                arrive(cond, h, piece)
                send(onward, g_copy(h, piece, to, lane))
                send(cond, g_copy(h, piece, y_mate, 2))
                send(cond, g_copy(h, piece, c_mate, 3))
        if d == 1:
            y_arrived(None, z)
        else:
            y_arrived(z >= d - 1, clamp(z - d + 1))
            y_arrived(z + d - 1 <= 3, clamp(z + d - 1))
        work()
        for cond, zz, _, _, _ in ways:
            ready.append((cond, index(zz, y, core)))
    y_arrived(z >= 3, clamp(z - 3))
    y_arrived(z <= 0, clamp(z + 3))
    work()

    def others(i, carry):
        piece = index(i // 2, lax.rem(i, 2), 1 - core)
        for h in range(per):
            arrive(None, h, piece)
        first(piece)
        return carry

    lax.fori_loop(0, n // 2, others, 0)

    table_copy.wait()
    pitch = trace.shape[1] // rows
    pk[...] = jnp.zeros_like(pk)
    step = 4
    lanes = pk.shape[1]

    def second(i, carry):
        parts = [cross[i * step + q].reshape(2 * groups * GROUP, rows).T for q in range(step)]
        out = jnp.dot(
            jnp.concatenate(parts, axis=0), table_ref[...], preferred_element_type=jnp.float32
        )
        best = pk[...]
        for q in range(step):
            piece = out[q * rows:(q + 1) * rows]
            for c in range(LAGS // lanes):
                part = piece[:, c * lanes:(c + 1) * lanes]
                trace[c, pl.ds(i * step + q, rows, stride=pitch), :] = part
                best = jnp.maximum(best, jnp.abs(part))
        pk[...] = best
        return carry

    lax.fori_loop(0, receivers // step, second, 0)

    own = jnp.max(pk[...].T, axis=0, keepdims=True)
    slots[me] = jnp.broadcast_to(own, slots.shape[1:])

    def p_copy(off):
        return pltpu.make_async_remote_copy(
            src_ref=slots.at[me], dst_ref=slots.at[me], send_sem=p_send.at[off],
            recv_sem=p_recv.at[me], device_id=at_chan(lax.rem(me + off, n)),
            device_id_type=mesh_ids,
        )

    for off in range(1, n):
        p_copy(off).start()
    for h in range(per):
        for off in range(1, n):
            a_copy(h, off).wait_send()
    for cond, copy in sent:
        guarded(cond, copy.wait_send)
    for off in range(1, n):
        frm = lax.rem(me + n - off, n)
        pltpu.make_async_remote_copy(
            src_ref=slots.at[frm], dst_ref=slots.at[frm], send_sem=p_send.at[off],
            recv_sem=p_recv.at[frm], device_id=at_chan(frm), device_id_type=mesh_ids,
        ).wait_recv()
    top = jnp.max(jnp.max(slots[...], axis=0), axis=0, keepdims=True)
    inverse[...] = 1.0 / (jnp.broadcast_to(top, inverse.shape).T + 1e-06)

    block = rows // o_sem.shape[0]
    size = block * receivers

    def o_copy(i):
        here = pl.ds(pl.multiple_of(i * size, size), size)
        return pltpu.make_async_copy(stage.at[here], out_ref.at[here], o_sem.at[i])

    def finish(i, carry):
        for q in range(block):
            row = i * block + q
            factor = inverse[pl.ds(row, 1), :]
            here = pl.ds(pl.multiple_of(row * receivers, receivers), receivers)
            held_at = pl.ds(pl.multiple_of(row * pitch, 8), receivers)
            for c in range(LAGS // lanes):
                stage[here, c * lanes:(c + 1) * lanes] = (trace[c, held_at, :] * factor).astype(
                    jnp.bfloat16
                )
        o_copy(i).start()
        return carry

    lax.fori_loop(0, o_sem.shape[0], finish, 0)
    for off in range(1, n):
        p_copy(off).wait_send()
    for i in range(o_sem.shape[0]):
        o_copy(i).wait()


def reorder_rows(receivers, windows):
    ch, w = np.meshgrid(np.arange(receivers), np.arange(windows), indexing="ij")
    rows = np.zeros((receivers * windows,) * 2, np.float32)
    rows[(w * receivers + ch).ravel(), (ch * windows + w).ravel()] = 1.0
    return rows.astype(ml_dtypes.bfloat16)


def fused(n, spectra, blocks, valid, table):
    receivers, windows, width = spectra.shape
    groups = width // 2 // GROUP
    depth = 2 * windows * GROUP
    sources = 4 * SOURCE
    chunks = 8
    per = groups // n
    vmem = pl.BlockSpec(memory_space=pltpu.VMEM)
    smem = pl.BlockSpec(memory_space=pltpu.SMEM)
    by_row = reorder_rows(receivers, windows)
    dma = pltpu.SemaphoreType.DMA
    return pl.pallas_call(
        functools.partial(fused_kernel, n),
        out_shape=jax.ShapeDtypeStruct((sources * receivers, LAGS), jnp.bfloat16),
        in_specs=[vmem, smem, smem, vmem, pl.BlockSpec(memory_space=pl.ANY)],
        out_specs=pl.BlockSpec(memory_space=pl.ANY),
        scratch_shapes=[
            pltpu.VMEM(table.shape, table.dtype),
            pltpu.VMEM((groups, receivers, depth), jnp.bfloat16),
            pltpu.VMEM((n, receivers, depth), jnp.bfloat16),
            pltpu.VMEM((n, receivers, depth), jnp.bfloat16),
            pltpu.VMEM((groups, sources, depth), jnp.bfloat16),
            pltpu.VMEM((groups, receivers * 2 * GROUP, depth), jnp.bfloat16),
            pltpu.VMEM((receivers, 2, groups * GROUP, sources), jnp.bfloat16),
            pltpu.VMEM((LAGS // 128, sources * (receivers + 8), 128), jnp.float32),
            pltpu.VMEM((sources * receivers, LAGS), jnp.bfloat16),
            pltpu.VMEM((sources, 128), jnp.float32),
            pltpu.VMEM((n, 8, sources), jnp.float32),
            pltpu.VMEM((sources, 128), jnp.float32),
            dma((per, n)),
            dma((per, n)),
            dma((per, 4, n)),
            dma((per, n)),
            dma((n,)),
            dma((n,)),
            dma((chunks,)),
            dma(()),
        ],
        compiler_params=pltpu.CompilerParams(
            collective_id=0, has_side_effects=True, vmem_limit_bytes=VMEM_LIMIT
        ),
        name="fused",
    )(
        spectra.reshape(receivers * windows, width), blocks, valid,
        jnp.asarray(by_row), table,
    )


def correlate_kernel(s_ref, x_ref, table_ref, trace_ref, peak_ref, cross, pk):
    groups, rows, depth = s_ref.shape
    receivers = x_ref.shape[1]
    half = depth // 2
    diag = lax.rem(lax.broadcasted_iota(jnp.int32, (GROUP, depth), 1), GROUP) == (
        lax.broadcasted_iota(jnp.int32, (GROUP, depth), 0)
    )

    def first(g, carry):
        v = x_ref[g].astype(jnp.float32)
        turned = jnp.concatenate([v[:, half:], -v[:, :half]], axis=1)
        both = jnp.stack([v, turned], axis=1)
        spread = jnp.where(diag[None, None], both[:, :, None, :], 0.0).astype(jnp.bfloat16)
        spread = spread.reshape(receivers * 2 * GROUP, depth)
        out = lax.dot_general(
            spread, s_ref[g], (((1,), (1,)), ((), ())), preferred_element_type=jnp.float32
        ).astype(jnp.bfloat16)
        where = pl.ds(pl.multiple_of(g * GROUP, GROUP), GROUP)
        cross[:, :, where, :] = out.reshape(receivers, 2, GROUP, rows)
        return carry

    lax.fori_loop(0, groups, first, 0)

    pk[...] = jnp.zeros_like(pk)
    step = 4
    lanes = pk.shape[1]

    def second(i, carry):
        parts = [
            cross[i * step + q].reshape(2 * groups * GROUP, rows).T for q in range(step)
        ]
        out = jnp.dot(
            jnp.concatenate(parts, axis=0), table_ref[...], preferred_element_type=jnp.float32
        )
        best = pk[...]
        for q in range(step):
            piece = out[q * rows:(q + 1) * rows]
            for c in range(LAGS // lanes):
                cols = piece[:, c * lanes:(c + 1) * lanes]
                trace_ref[c, pl.ds(i * step + q, rows, stride=receivers), :] = cols
                best = jnp.maximum(best, jnp.abs(cols))
        pk[...] = best
        return carry

    lax.fori_loop(0, receivers // step, second, 0)
    peak_ref[...] = jnp.broadcast_to(jnp.max(pk[...].T, axis=0, keepdims=True), peak_ref.shape)


def correlate(sources, x, table):
    groups, rows, depth = sources.shape
    receivers = x.shape[1]
    vmem = pl.BlockSpec(memory_space=pltpu.VMEM)
    return pl.pallas_call(
        correlate_kernel,
        out_shape=(
            jax.ShapeDtypeStruct((LAGS // 128, rows * receivers, 128), jnp.float32),
            jax.ShapeDtypeStruct((8, rows), jnp.float32),
        ),
        in_specs=[vmem] * 3,
        out_specs=(vmem, vmem),
        scratch_shapes=[
            pltpu.VMEM((receivers, 2, groups * GROUP, rows), jnp.bfloat16),
            pltpu.VMEM((rows, 128), jnp.float32),
        ],
        compiler_params=pltpu.CompilerParams(vmem_limit_bytes=VMEM_LIMIT),
        name="correlate",
    )(sources, x, table)


def scale_kernel(block, receivers, peak_ref, trace_ref, out_ref):
    i = pl.program_id(0)
    for q in range(block):
        peak = jnp.full((1, 128), peak_ref[0, i * block + q], jnp.float32)
        inverse = 1.0 / (peak + 1e-06)
        here = slice(q * receivers, (q + 1) * receivers)
        for c in range(LAGS // 128):
            cols = slice(c * 128, (c + 1) * 128)
            out_ref[here, cols] = (trace_ref[c, here, :] * inverse).astype(jnp.bfloat16)


def scale(trace, peak, receivers):
    block = 16
    total = trace.shape[1]
    steps = total // (block * receivers)
    return pl.pallas_call(
        functools.partial(scale_kernel, block, receivers),
        out_shape=jax.ShapeDtypeStruct((total, LAGS), jnp.bfloat16),
        grid=(steps,),
        in_specs=[
            pl.BlockSpec(memory_space=pltpu.SMEM),
            pl.BlockSpec((LAGS // 128, block * receivers, 128), lambda i: (0, i, 0)),
        ],
        out_specs=pl.BlockSpec((block * receivers, LAGS), lambda i: (i, 0)),
        compiler_params=pltpu.CompilerParams(vmem_limit_bytes=VMEM_LIMIT),
        name="scale",
    )(peak, trace)


def shards(n, spectra, source_blocks, window_valid):
    receivers, windows, width = spectra.shape
    bins = width // 2
    groups = bins // GROUP
    num_steps = source_blocks.shape[0]
    table = jnp.asarray(build_table(bins, LAGS))
    if n == 16:
        out = fused(n, spectra, source_blocks, window_valid, table)
    else:
        x = spectra.reshape(receivers, windows, 2, groups, GROUP).transpose(3, 0, 2, 1, 4)
        x = x.reshape(groups, receivers, 2 * windows * GROUP)
        mask = jnp.tile(jnp.repeat(window_valid.astype(jnp.bfloat16), GROUP), 2)[None, :]
        roots = source_blocks.reshape(-1) // (receivers // SOURCE)
        mine = (roots == lax.axis_index("chan"))[None, :, None, None]
        picked = jnp.where(mine, (x * mask)[:, None], jnp.zeros((), x.dtype))
        sources = lax.psum(picked.reshape(groups, -1, x.shape[2]), "chan")
        trace, peak = correlate(sources, x, table)
        out = scale(trace, lax.pmax(peak, "chan"), receivers)
    return out.reshape(num_steps, 2, SOURCE, receivers, LAGS)


def solution(mesh):
    placed = (P(("parts", "chan"), None, None), P("parts", None), P("parts"))
    return jax.shard_map(
        functools.partial(shards, mesh.shape["chan"]),
        mesh=mesh,
        in_specs=placed,
        out_specs=P(None, None, None, ("parts", "chan"), None),
        check_vma=False,
    )
```

```python
import functools
import math

import jax
import jax.numpy as jnp
import ml_dtypes
import numpy as np
from jax import lax
from jax.experimental import pallas as pl
from jax.experimental.pallas import tpu as pltpu
from jax.sharding import PartitionSpec as P

SOURCE = 32
LAGS = 512
GROUP = 16
VMEM_LIMIT = 56 * 1024 * 1024


def build_table(bins, lags):
    freq = np.arange(bins)[:, None]
    shifted = np.arange(lags)[None, :] - lags // 2
    theta = np.remainder(freq * shifted, 2 * bins) * (2.0 * math.pi / (2 * bins))
    weight = np.where(freq == 0, 1.0, 2.0) / (2 * bins)
    table = np.concatenate([weight * np.cos(theta), -weight * np.sin(theta)], axis=0)
    return table.astype(np.float32).astype(ml_dtypes.bfloat16)


def at_chan(index):
    return {"chan": index}


def fused_kernel(
    n, a_ref, blocks_ref, valid_ref, rows_ref, table_hbm, out_ref,
    table_ref, x, cand0, cand1, held, spread, cross, acc, trace, stage, pk, slots, inverse,
    a_send, a_recv, g_send, g_recv, p_send, p_recv, o_sem, t_sem,
):
    me = lax.axis_index("chan")
    z = me // 4
    y = lax.rem(me // 2, 2)
    core = lax.rem(me, 2)
    groups, receivers, depth = x.shape
    per = groups // n
    half = depth // 2
    rows = held.shape[1]
    mesh_ids = pl.DeviceIdType.MESH
    cand = (cand0, cand1)

    table_copy = pltpu.make_async_copy(table_hbm, table_ref, t_sem)
    table_copy.start()
    barrier = pltpu.get_barrier_semaphore()
    for off in range(1, n):
        pl.semaphore_signal(
            barrier, inc=1, device_id=at_chan(lax.rem(me + off, n)), device_id_type=mesh_ids
        )

    low = half // GROUP
    row = lax.broadcasted_iota(jnp.int32, (depth * 4, half), 0)
    lane = lax.broadcasted_iota(jnp.int32, (depth * 4, half), 1)
    target = (row // half) * GROUP + lax.rem(row, GROUP)
    here = lane == target
    belongs = lax.rem(row, half) // GROUP
    cols = jnp.concatenate(
        [
            jnp.where(jnp.logical_and(here, belongs == t), 1.0, 0.0).astype(jnp.bfloat16)
            for t in range(low)
        ],
        axis=1,
    )

    by_window = jnp.dot(
        rows_ref[...], a_ref[...], preferred_element_type=jnp.float32
    ).astype(jnp.bfloat16)
    windows = by_window.shape[0] // receivers
    tiles = by_window.shape[1] // half
    flat = jnp.concatenate(
        [
            jnp.concatenate(
                [
                    by_window[w * receivers:(w + 1) * receivers, t * half:(t + 1) * half]
                    for w in range(windows)
                ],
                axis=1,
            )
            for t in range(tiles)
        ],
        axis=0,
    )
    turned = jnp.dot(flat, cols, preferred_element_type=jnp.float32).astype(jnp.bfloat16)
    high = tiles // 2
    for t in range(tiles):
        c, gh = t // high, t % high
        for gl in range(low):
            x[gh * low + gl, :, c * half:(c + 1) * half] = turned[
                t * receivers:(t + 1) * receivers, gl * half:(gl + 1) * half
            ]

    pl.semaphore_wait(barrier, n - 1)

    def a_copy(h, off):
        to = lax.rem(me + off, n)
        return pltpu.make_async_remote_copy(
            src_ref=x.at[to * per + h], dst_ref=cand[h].at[me],
            send_sem=a_send.at[h, off], recv_sem=a_recv.at[h, me],
            device_id=at_chan(to), device_id_type=mesh_ids,
        )

    for h in range(per):
        for off in range(1, n):
            a_copy(h, off).start()
    for h in range(per):
        cand[h][me] = x[me * per + h]

    diag = lax.rem(lax.broadcasted_iota(jnp.int32, (GROUP, depth), 1), GROUP) == (
        lax.broadcasted_iota(jnp.int32, (GROUP, depth), 0)
    )

    def widen(g, carry):
        v = x[g].astype(jnp.float32)
        rotated = jnp.concatenate([v[:, half:], -v[:, :half]], axis=1)
        both = jnp.stack([v, rotated], axis=1)
        wide = jnp.where(diag[None, None], both[:, :, None, :], 0.0).astype(jnp.bfloat16)
        spread[g] = wide.reshape(receivers * 2 * GROUP, depth)
        return carry

    lax.fori_loop(0, groups, widen, 0)

    window = lax.rem(lax.broadcasted_iota(jnp.int32, (1, depth), 1), half) // GROUP
    mask = jnp.zeros((1, depth), jnp.float32)
    for w in range(windows):
        mask = jnp.where(window == w, valid_ref[w].astype(jnp.float32), mask)
    mask = mask.astype(jnp.bfloat16)

    def index(zz, yy, cc):
        return (zz * 2 + yy) * 2 + cc

    def g_copy(h, piece, to, lane):
        ref = held.at[piece * per + h]
        return pltpu.make_async_remote_copy(
            src_ref=ref, dst_ref=ref, send_sem=g_send.at[h, lane, piece],
            recv_sem=g_recv.at[h, piece], device_id=at_chan(to), device_id_type=mesh_ids,
        )

    y_mate = index(z, 1 - y, core)
    c_mate = index(z, y, 1 - core)
    up = lax.rem(me + 4, n)
    down = lax.rem(me + n - 4, n)
    sent = []

    def guarded(cond, action):
        if cond is None:
            action()
        else:
            pl.when(cond)(action)

    def send(cond, copy):
        sent.append((cond, copy))
        guarded(cond, copy.start)

    def arrive(cond, h, piece):
        guarded(cond, g_copy(h, piece, c_mate, 0).wait_recv)

    table_copy.wait()
    pitch = trace.shape[1] // rows
    step = acc.shape[1] // rows
    lanes = pk.shape[1]
    bundle = groups // 4

    def plane(q, mode):
        for yy in range(2):
            for h in range(per):
                arrive(None, h, index(q, yy, 1 - core))

        def first(j, carry):
            g = q * bundle + j
            out = lax.dot_general(
                spread[g], held[g], (((1,), (1,)), ((), ())), preferred_element_type=jnp.float32
            ).astype(jnp.bfloat16)
            where = pl.ds(pl.multiple_of(j * GROUP, GROUP), GROUP)
            cross[:, :, where, :] = out.reshape(receivers, 2, GROUP, rows)
            return carry

        lax.fori_loop(0, bundle, first, 0)

        def second(i, carry):
            parts = [
                cross[i * step + r].reshape(2 * bundle * GROUP, rows).T for r in range(step)
            ]
            out = jnp.dot(
                jnp.concatenate(parts, axis=0), table_ref[q], preferred_element_type=jnp.float32
            )
            if mode == "init":
                acc[i] = out
            elif mode == "add":
                acc[i] += out
            else:
                out = out + acc[i]
                best = pk[...]
                for r in range(step):
                    for c in range(LAGS // lanes):
                        part = out[r * rows:(r + 1) * rows, c * lanes:(c + 1) * lanes]
                        trace[c, pl.ds(i * step + r, rows, stride=pitch), :] = part
                        best = jnp.maximum(best, jnp.abs(part))
                pk[...] = best
            return carry

        lax.fori_loop(0, receivers // step, second, 0)

    for h in range(per):
        for off in range(1, n):
            frm = lax.rem(me + n - off, n)
            pltpu.make_async_remote_copy(
                src_ref=cand[h].at[frm], dst_ref=cand[h].at[frm],
                send_sem=a_send.at[h, off], recv_sem=a_recv.at[h, frm],
                device_id=at_chan(frm), device_id_type=mesh_ids,
            ).wait_recv()
        for k in range(4):
            b = blocks_ref[k // 2, k % 2]
            held[me * per + h, SOURCE * k:SOURCE * (k + 1), :] = cand[h][b] * mask
        send(z < 3, g_copy(h, me, up, 0))
        send(z > 0, g_copy(h, me, down, 1))
        send(None, g_copy(h, me, y_mate, 2))
        send(None, g_copy(h, me, c_mate, 3))

    def clamp(zz):
        return jnp.clip(zz, 0, 3)

    def y_arrived(cond, zz):
        piece = index(zz, 1 - y, core)
        for h in range(per):
            arrive(cond, h, piece)
            send(cond, g_copy(h, piece, c_mate, 3))

    for d in range(1, 4):
        low_in, low_z = z >= d, clamp(z - d)
        high_in, high_z = z + d <= 3, clamp(z + d)
        ways = (
            (low_in, low_z, jnp.logical_and(low_in, z < 3), up, 0),
            (high_in, high_z, jnp.logical_and(high_in, z > 0), down, 1),
        )
        for h in range(per):
            for cond, zz, onward, to, lane in ways:
                piece = index(zz, y, core)
                arrive(cond, h, piece)
                send(onward, g_copy(h, piece, to, lane))
                send(cond, g_copy(h, piece, y_mate, 2))
                send(cond, g_copy(h, piece, c_mate, 3))
        if d == 1:
            y_arrived(None, z)
            plane(z, "init")
        else:
            y_arrived(z >= d - 1, clamp(z - d + 1))
            y_arrived(z + d - 1 <= 3, clamp(z + d - 1))
        if d == 2:
            pl.when(z >= 1)(functools.partial(plane, clamp(z - 1), "add"))
            pl.when(z <= 2)(functools.partial(plane, clamp(z + 1), "add"))
        if d == 3:
            pl.when(z == 0)(functools.partial(plane, clamp(z + 2), "add"))
            pl.when(z == 3)(functools.partial(plane, clamp(z - 2), "add"))
    y_arrived(z >= 3, clamp(z - 3))
    y_arrived(z <= 0, clamp(z + 3))
    pk[...] = jnp.zeros_like(pk)
    plane(3 - 3 * (z // 2), "last")

    own = jnp.max(pk[...].T, axis=0, keepdims=True)
    slots[me] = jnp.broadcast_to(own, slots.shape[1:])

    def p_copy(off):
        return pltpu.make_async_remote_copy(
            src_ref=slots.at[me], dst_ref=slots.at[me], send_sem=p_send.at[off],
            recv_sem=p_recv.at[me], device_id=at_chan(lax.rem(me + off, n)),
            device_id_type=mesh_ids,
        )

    for off in range(1, n):
        p_copy(off).start()
    for h in range(per):
        for off in range(1, n):
            a_copy(h, off).wait_send()
    for cond, copy in sent:
        guarded(cond, copy.wait_send)
    for off in range(1, n):
        frm = lax.rem(me + n - off, n)
        pltpu.make_async_remote_copy(
            src_ref=slots.at[frm], dst_ref=slots.at[frm], send_sem=p_send.at[off],
            recv_sem=p_recv.at[frm], device_id=at_chan(frm), device_id_type=mesh_ids,
        ).wait_recv()
    top = jnp.max(jnp.max(slots[...], axis=0), axis=0, keepdims=True)
    inverse[...] = 1.0 / (jnp.broadcast_to(top, inverse.shape).T + 1e-06)

    block = rows // o_sem.shape[0]
    size = block * receivers

    def o_copy(i):
        here = pl.ds(pl.multiple_of(i * size, size), size)
        return pltpu.make_async_copy(stage.at[here], out_ref.at[here], o_sem.at[i])

    def finish(i, carry):
        for q in range(block):
            row = i * block + q
            factor = inverse[pl.ds(row, 1), :]
            here = pl.ds(pl.multiple_of(row * receivers, receivers), receivers)
            held_at = pl.ds(pl.multiple_of(row * pitch, 8), receivers)
            for c in range(LAGS // lanes):
                stage[here, c * lanes:(c + 1) * lanes] = (trace[c, held_at, :] * factor).astype(
                    jnp.bfloat16
                )
        o_copy(i).start()
        return carry

    lax.fori_loop(0, o_sem.shape[0], finish, 0)
    for off in range(1, n):
        p_copy(off).wait_send()
    for i in range(o_sem.shape[0]):
        o_copy(i).wait()


def reorder_rows(receivers, windows):
    ch, w = np.meshgrid(np.arange(receivers), np.arange(windows), indexing="ij")
    rows = np.zeros((receivers * windows,) * 2, np.float32)
    rows[(w * receivers + ch).ravel(), (ch * windows + w).ravel()] = 1.0
    return rows.astype(ml_dtypes.bfloat16)


def fused(n, spectra, blocks, valid, table):
    receivers, windows, width = spectra.shape
    groups = width // 2 // GROUP
    depth = 2 * windows * GROUP
    sources = 4 * SOURCE
    chunks = 8
    per = groups // n
    vmem = pl.BlockSpec(memory_space=pltpu.VMEM)
    smem = pl.BlockSpec(memory_space=pltpu.SMEM)
    by_row = reorder_rows(receivers, windows)
    dma = pltpu.SemaphoreType.DMA
    return pl.pallas_call(
        functools.partial(fused_kernel, n),
        out_shape=jax.ShapeDtypeStruct((sources * receivers, LAGS), jnp.bfloat16),
        in_specs=[vmem, smem, smem, vmem, pl.BlockSpec(memory_space=pl.ANY)],
        out_specs=pl.BlockSpec(memory_space=pl.ANY),
        scratch_shapes=[
            pltpu.VMEM(table.shape, table.dtype),
            pltpu.VMEM((groups, receivers, depth), jnp.bfloat16),
            pltpu.VMEM((n, receivers, depth), jnp.bfloat16),
            pltpu.VMEM((n, receivers, depth), jnp.bfloat16),
            pltpu.VMEM((groups, sources, depth), jnp.bfloat16),
            pltpu.VMEM((groups, receivers * 2 * GROUP, depth), jnp.bfloat16),
            pltpu.VMEM((receivers, 2, groups // 4 * GROUP, sources), jnp.bfloat16),
            pltpu.VMEM((receivers // 4, 4 * sources, LAGS), jnp.float32),
            pltpu.VMEM((LAGS // 128, sources * (receivers + 8), 128), jnp.float32),
            pltpu.VMEM((sources * receivers, LAGS), jnp.bfloat16),
            pltpu.VMEM((sources, 128), jnp.float32),
            pltpu.VMEM((n, 8, sources), jnp.float32),
            pltpu.VMEM((sources, 128), jnp.float32),
            dma((per, n)),
            dma((per, n)),
            dma((per, 4, n)),
            dma((per, n)),
            dma((n,)),
            dma((n,)),
            dma((chunks,)),
            dma(()),
        ],
        compiler_params=pltpu.CompilerParams(
            collective_id=0, has_side_effects=True, vmem_limit_bytes=VMEM_LIMIT
        ),
        name="fused",
    )(
        spectra.reshape(receivers * windows, width), blocks, valid,
        jnp.asarray(by_row), table,
    )


def correlate_kernel(s_ref, x_ref, table_ref, trace_ref, peak_ref, cross, pk):
    groups, rows, depth = s_ref.shape
    receivers = x_ref.shape[1]
    half = depth // 2
    diag = lax.rem(lax.broadcasted_iota(jnp.int32, (GROUP, depth), 1), GROUP) == (
        lax.broadcasted_iota(jnp.int32, (GROUP, depth), 0)
    )

    def first(g, carry):
        v = x_ref[g].astype(jnp.float32)
        turned = jnp.concatenate([v[:, half:], -v[:, :half]], axis=1)
        both = jnp.stack([v, turned], axis=1)
        spread = jnp.where(diag[None, None], both[:, :, None, :], 0.0).astype(jnp.bfloat16)
        spread = spread.reshape(receivers * 2 * GROUP, depth)
        out = lax.dot_general(
            spread, s_ref[g], (((1,), (1,)), ((), ())), preferred_element_type=jnp.float32
        ).astype(jnp.bfloat16)
        where = pl.ds(pl.multiple_of(g * GROUP, GROUP), GROUP)
        cross[:, :, where, :] = out.reshape(receivers, 2, GROUP, rows)
        return carry

    lax.fori_loop(0, groups, first, 0)

    pk[...] = jnp.zeros_like(pk)
    step = 4
    lanes = pk.shape[1]

    def second(i, carry):
        parts = [
            cross[i * step + q].reshape(2 * groups * GROUP, rows).T for q in range(step)
        ]
        out = jnp.dot(
            jnp.concatenate(parts, axis=0), table_ref[...], preferred_element_type=jnp.float32
        )
        best = pk[...]
        for q in range(step):
            piece = out[q * rows:(q + 1) * rows]
            for c in range(LAGS // lanes):
                cols = piece[:, c * lanes:(c + 1) * lanes]
                trace_ref[c, pl.ds(i * step + q, rows, stride=receivers), :] = cols
                best = jnp.maximum(best, jnp.abs(cols))
        pk[...] = best
        return carry

    lax.fori_loop(0, receivers // step, second, 0)
    peak_ref[...] = jnp.broadcast_to(jnp.max(pk[...].T, axis=0, keepdims=True), peak_ref.shape)


def correlate(sources, x, table):
    groups, rows, depth = sources.shape
    receivers = x.shape[1]
    vmem = pl.BlockSpec(memory_space=pltpu.VMEM)
    return pl.pallas_call(
        correlate_kernel,
        out_shape=(
            jax.ShapeDtypeStruct((LAGS // 128, rows * receivers, 128), jnp.float32),
            jax.ShapeDtypeStruct((8, rows), jnp.float32),
        ),
        in_specs=[vmem] * 3,
        out_specs=(vmem, vmem),
        scratch_shapes=[
            pltpu.VMEM((receivers, 2, groups * GROUP, rows), jnp.bfloat16),
            pltpu.VMEM((rows, 128), jnp.float32),
        ],
        compiler_params=pltpu.CompilerParams(vmem_limit_bytes=VMEM_LIMIT),
        name="correlate",
    )(sources, x, table)


def scale_kernel(block, receivers, peak_ref, trace_ref, out_ref):
    i = pl.program_id(0)
    for q in range(block):
        peak = jnp.full((1, 128), peak_ref[0, i * block + q], jnp.float32)
        inverse = 1.0 / (peak + 1e-06)
        here = slice(q * receivers, (q + 1) * receivers)
        for c in range(LAGS // 128):
            cols = slice(c * 128, (c + 1) * 128)
            out_ref[here, cols] = (trace_ref[c, here, :] * inverse).astype(jnp.bfloat16)


def scale(trace, peak, receivers):
    block = 16
    total = trace.shape[1]
    steps = total // (block * receivers)
    return pl.pallas_call(
        functools.partial(scale_kernel, block, receivers),
        out_shape=jax.ShapeDtypeStruct((total, LAGS), jnp.bfloat16),
        grid=(steps,),
        in_specs=[
            pl.BlockSpec(memory_space=pltpu.SMEM),
            pl.BlockSpec((LAGS // 128, block * receivers, 128), lambda i: (0, i, 0)),
        ],
        out_specs=pl.BlockSpec((block * receivers, LAGS), lambda i: (i, 0)),
        compiler_params=pltpu.CompilerParams(vmem_limit_bytes=VMEM_LIMIT),
        name="scale",
    )(peak, trace)


def shards(n, spectra, source_blocks, window_valid):
    receivers, windows, width = spectra.shape
    bins = width // 2
    groups = bins // GROUP
    num_steps = source_blocks.shape[0]
    table = jnp.asarray(build_table(bins, LAGS))
    if n == 16:
        by_plane = build_table(bins, LAGS).reshape(2, 4, bins // 4, LAGS).transpose(1, 0, 2, 3)
        by_plane = jnp.asarray(by_plane.reshape(4, bins // 2, LAGS))
        out = fused(n, spectra, source_blocks, window_valid, by_plane)
    else:
        x = spectra.reshape(receivers, windows, 2, groups, GROUP).transpose(3, 0, 2, 1, 4)
        x = x.reshape(groups, receivers, 2 * windows * GROUP)
        mask = jnp.tile(jnp.repeat(window_valid.astype(jnp.bfloat16), GROUP), 2)[None, :]
        roots = source_blocks.reshape(-1) // (receivers // SOURCE)
        mine = (roots == lax.axis_index("chan"))[None, :, None, None]
        picked = jnp.where(mine, (x * mask)[:, None], jnp.zeros((), x.dtype))
        sources = lax.psum(picked.reshape(groups, -1, x.shape[2]), "chan")
        trace, peak = correlate(sources, x, table)
        out = scale(trace, lax.pmax(peak, "chan"), receivers)
    return out.reshape(num_steps, 2, SOURCE, receivers, LAGS)


def solution(mesh):
    placed = (P(("parts", "chan"), None, None), P("parts", None), P("parts"))
    return jax.shard_map(
        functools.partial(shards, mesh.shape["chan"]),
        mesh=mesh,
        in_specs=placed,
        out_specs=P(None, None, None, ("parts", "chan"), None),
        check_vma=False,
    )
```

```python
import functools
import math

import jax
import jax.numpy as jnp
import ml_dtypes
import numpy as np
from jax import lax
from jax.experimental import pallas as pl
from jax.experimental.pallas import tpu as pltpu
from jax.sharding import PartitionSpec as P

SOURCE = 32
LAGS = 512
GROUP = 16
VMEM_LIMIT = 56 * 1024 * 1024


def build_table(bins, lags):
    freq = np.arange(bins)[:, None]
    shifted = np.arange(lags)[None, :] - lags // 2
    theta = np.remainder(freq * shifted, 2 * bins) * (2.0 * math.pi / (2 * bins))
    weight = np.where(freq == 0, 1.0, 2.0) / (2 * bins)
    table = np.concatenate([weight * np.cos(theta), -weight * np.sin(theta)], axis=0)
    return table.astype(np.float32).astype(ml_dtypes.bfloat16)


def at_chan(index):
    return {"chan": index}


def fused_kernel(
    n, a_ref, blocks_ref, valid_ref, rows_ref, table_hbm, out_ref,
    table_ref, x, cand0, cand1, held, spread, cross, trace, stage, pk, slots, inverse,
    a_send, a_recv, g_send, g_recv, p_send, p_recv, o_sem, t_sem,
):
    me = lax.axis_index("chan")
    z = me // 4
    y = lax.rem(me // 2, 2)
    core = lax.rem(me, 2)
    groups, receivers, depth = x.shape
    per = groups // n
    half = depth // 2
    rows = held.shape[1]
    mesh_ids = pl.DeviceIdType.MESH
    cand = (cand0, cand1)

    table_copy = pltpu.make_async_copy(table_hbm, table_ref, t_sem)
    table_copy.start()
    barrier = pltpu.get_barrier_semaphore()
    for off in range(1, n):
        pl.semaphore_signal(
            barrier, inc=1, device_id=at_chan(lax.rem(me + off, n)), device_id_type=mesh_ids
        )

    low = half // GROUP
    row = lax.broadcasted_iota(jnp.int32, (depth * 4, half), 0)
    lane = lax.broadcasted_iota(jnp.int32, (depth * 4, half), 1)
    target = (row // half) * GROUP + lax.rem(row, GROUP)
    here = lane == target
    belongs = lax.rem(row, half) // GROUP
    cols = jnp.concatenate(
        [
            jnp.where(jnp.logical_and(here, belongs == t), 1.0, 0.0).astype(jnp.bfloat16)
            for t in range(low)
        ],
        axis=1,
    )

    by_window = jnp.dot(
        rows_ref[...], a_ref[...], preferred_element_type=jnp.float32
    ).astype(jnp.bfloat16)
    windows = by_window.shape[0] // receivers
    tiles = by_window.shape[1] // half
    flat = jnp.concatenate(
        [
            jnp.concatenate(
                [
                    by_window[w * receivers:(w + 1) * receivers, t * half:(t + 1) * half]
                    for w in range(windows)
                ],
                axis=1,
            )
            for t in range(tiles)
        ],
        axis=0,
    )
    turned = jnp.dot(flat, cols, preferred_element_type=jnp.float32).astype(jnp.bfloat16)
    high = tiles // 2
    for t in range(tiles):
        c, gh = t // high, t % high
        for gl in range(low):
            x[gh * low + gl, :, c * half:(c + 1) * half] = turned[
                t * receivers:(t + 1) * receivers, gl * half:(gl + 1) * half
            ]

    pl.semaphore_wait(barrier, n - 1)

    def a_copy(h, off):
        to = lax.rem(me + off, n)
        return pltpu.make_async_remote_copy(
            src_ref=x.at[to * per + h], dst_ref=cand[h].at[me],
            send_sem=a_send.at[h, off], recv_sem=a_recv.at[h, me],
            device_id=at_chan(to), device_id_type=mesh_ids,
        )

    for h in range(per):
        for off in range(1, n):
            a_copy(h, off).start()
    for h in range(per):
        cand[h][me] = x[me * per + h]

    diag = lax.rem(lax.broadcasted_iota(jnp.int32, (GROUP, depth), 1), GROUP) == (
        lax.broadcasted_iota(jnp.int32, (GROUP, depth), 0)
    )

    def widen(g, carry):
        v = x[g].astype(jnp.float32)
        rotated = jnp.concatenate([v[:, half:], -v[:, :half]], axis=1)
        both = jnp.stack([v, rotated], axis=1)
        wide = jnp.where(diag[None, None], both[:, :, None, :], 0.0).astype(jnp.bfloat16)
        spread[g] = wide.reshape(receivers * 2 * GROUP, depth)
        return carry

    lax.fori_loop(0, groups // 2, widen, 0)

    window = lax.rem(lax.broadcasted_iota(jnp.int32, (1, depth), 1), half) // GROUP
    mask = jnp.zeros((1, depth), jnp.float32)
    for w in range(windows):
        mask = jnp.where(window == w, valid_ref[w].astype(jnp.float32), mask)
    mask = mask.astype(jnp.bfloat16)

    def index(zz, yy, cc):
        return (zz * 2 + yy) * 2 + cc

    def g_copy(h, piece, to, lane):
        ref = held.at[piece * per + h]
        return pltpu.make_async_remote_copy(
            src_ref=ref, dst_ref=ref, send_sem=g_send.at[h, lane, piece],
            recv_sem=g_recv.at[h, piece], device_id=at_chan(to), device_id_type=mesh_ids,
        )

    y_mate = index(z, 1 - y, core)
    c_mate = index(z, y, 1 - core)
    up = lax.rem(me + 4, n)
    down = lax.rem(me + n - 4, n)
    sent = []

    def guarded(cond, action):
        if cond is None:
            action()
        else:
            pl.when(cond)(action)

    def send(cond, copy):
        sent.append((cond, copy))
        guarded(cond, copy.start)

    def arrive(cond, h, piece):
        guarded(cond, g_copy(h, piece, c_mate, 0).wait_recv)

    def first(piece):
        def body(h, carry):
            g = piece * per + h
            out = lax.dot_general(
                spread[g], held[g], (((1,), (1,)), ((), ())), preferred_element_type=jnp.float32
            ).astype(jnp.bfloat16)
            where = pl.ds(pl.multiple_of(g * GROUP, GROUP), GROUP)
            cross[:, :, where, :] = out.reshape(receivers, 2, GROUP, rows)
            return carry

        lax.fori_loop(0, per, body, 0)

    for h in range(per):
        for off in range(1, n):
            frm = lax.rem(me + n - off, n)
            pltpu.make_async_remote_copy(
                src_ref=cand[h].at[frm], dst_ref=cand[h].at[frm],
                send_sem=a_send.at[h, off], recv_sem=a_recv.at[h, frm],
                device_id=at_chan(frm), device_id_type=mesh_ids,
            ).wait_recv()
        for k in range(4):
            b = blocks_ref[k // 2, k % 2]
            held[me * per + h, SOURCE * k:SOURCE * (k + 1), :] = cand[h][b] * mask
        send(z < 3, g_copy(h, me, up, 0))
        send(z > 0, g_copy(h, me, down, 1))
        send(None, g_copy(h, me, y_mate, 2))
        send(None, g_copy(h, me, c_mate, 3))
        if h == 0:
            lax.fori_loop(groups // 2, groups, widen, 0)

    def clamp(zz):
        return jnp.clip(zz, 0, 3)

    ready = [(None, me)]

    def y_arrived(cond, zz):
        piece = index(zz, 1 - y, core)
        for h in range(per):
            arrive(cond, h, piece)
            send(cond, g_copy(h, piece, c_mate, 3))
        ready.append((cond, piece))

    def work():
        for cond, piece in ready:
            guarded(cond, functools.partial(first, piece))
        ready.clear()

    for d in range(1, 4):
        low_in, low_z = z >= d, clamp(z - d)
        high_in, high_z = z + d <= 3, clamp(z + d)
        ways = (
            (low_in, low_z, jnp.logical_and(low_in, z < 3), up, 0),
            (high_in, high_z, jnp.logical_and(high_in, z > 0), down, 1),
        )
        for h in range(per):
            for cond, zz, onward, to, lane in ways:
                piece = index(zz, y, core)
                arrive(cond, h, piece)
                send(onward, g_copy(h, piece, to, lane))
                send(cond, g_copy(h, piece, y_mate, 2))
                send(cond, g_copy(h, piece, c_mate, 3))
        if d == 1:
            y_arrived(None, z)
        else:
            y_arrived(z >= d - 1, clamp(z - d + 1))
            y_arrived(z + d - 1 <= 3, clamp(z + d - 1))
        work()
        for cond, zz, _, _, _ in ways:
            ready.append((cond, index(zz, y, core)))
    y_arrived(z >= 3, clamp(z - 3))
    y_arrived(z <= 0, clamp(z + 3))
    work()

    def others(i, carry):
        piece = index(i // 2, lax.rem(i, 2), 1 - core)
        for h in range(per):
            arrive(None, h, piece)
        first(piece)
        return carry

    lax.fori_loop(0, n // 2, others, 0)

    table_copy.wait()
    pitch = trace.shape[1] // rows
    pk[...] = jnp.zeros_like(pk)
    step = 8
    lanes = pk.shape[1]

    def second(i, carry):
        parts = [cross[i * step + q].reshape(2 * groups * GROUP, rows).T for q in range(step)]
        out = jnp.dot(
            jnp.concatenate(parts, axis=0), table_ref[...], preferred_element_type=jnp.float32
        )
        best = pk[...]
        for q in range(step):
            piece = out[q * rows:(q + 1) * rows]
            for c in range(LAGS // lanes):
                part = piece[:, c * lanes:(c + 1) * lanes]
                trace[c, pl.ds(i * step + q, rows, stride=pitch), :] = part
                best = jnp.maximum(best, jnp.abs(part))
        pk[...] = best
        return carry

    lax.fori_loop(0, receivers // step, second, 0)

    own = jnp.max(pk[...].T, axis=0, keepdims=True)
    slots[me] = jnp.broadcast_to(own, slots.shape[1:])

    def p_copy(off):
        return pltpu.make_async_remote_copy(
            src_ref=slots.at[me], dst_ref=slots.at[me], send_sem=p_send.at[off],
            recv_sem=p_recv.at[me], device_id=at_chan(lax.rem(me + off, n)),
            device_id_type=mesh_ids,
        )

    for off in range(1, n):
        p_copy(off).start()
    for h in range(per):
        for off in range(1, n):
            a_copy(h, off).wait_send()
    for cond, copy in sent:
        guarded(cond, copy.wait_send)
    for off in range(1, n):
        frm = lax.rem(me + n - off, n)
        pltpu.make_async_remote_copy(
            src_ref=slots.at[frm], dst_ref=slots.at[frm], send_sem=p_send.at[off],
            recv_sem=p_recv.at[frm], device_id=at_chan(frm), device_id_type=mesh_ids,
        ).wait_recv()
    top = jnp.max(jnp.max(slots[...], axis=0), axis=0, keepdims=True)
    inverse[...] = 1.0 / (jnp.broadcast_to(top, inverse.shape).T + 1e-06)

    block = rows // o_sem.shape[0]
    size = block * receivers

    def o_copy(i):
        here = pl.ds(pl.multiple_of(i * size, size), size)
        return pltpu.make_async_copy(stage.at[here], out_ref.at[here], o_sem.at[i])

    def finish(i, carry):
        for q in range(block):
            row = i * block + q
            factor = inverse[pl.ds(row, 1), :]
            here = pl.ds(pl.multiple_of(row * receivers, receivers), receivers)
            held_at = pl.ds(pl.multiple_of(row * pitch, 8), receivers)
            for c in range(LAGS // lanes):
                stage[here, c * lanes:(c + 1) * lanes] = (trace[c, held_at, :] * factor).astype(
                    jnp.bfloat16
                )
        o_copy(i).start()
        return carry

    lax.fori_loop(0, o_sem.shape[0], finish, 0)
    for off in range(1, n):
        p_copy(off).wait_send()
    for i in range(o_sem.shape[0]):
        o_copy(i).wait()


def reorder_rows(receivers, windows):
    ch, w = np.meshgrid(np.arange(receivers), np.arange(windows), indexing="ij")
    rows = np.zeros((receivers * windows,) * 2, np.float32)
    rows[(w * receivers + ch).ravel(), (ch * windows + w).ravel()] = 1.0
    return rows.astype(ml_dtypes.bfloat16)


def fused(n, spectra, blocks, valid, table):
    receivers, windows, width = spectra.shape
    groups = width // 2 // GROUP
    depth = 2 * windows * GROUP
    sources = 4 * SOURCE
    chunks = 8
    per = groups // n
    vmem = pl.BlockSpec(memory_space=pltpu.VMEM)
    smem = pl.BlockSpec(memory_space=pltpu.SMEM)
    by_row = reorder_rows(receivers, windows)
    dma = pltpu.SemaphoreType.DMA
    return pl.pallas_call(
        functools.partial(fused_kernel, n),
        out_shape=jax.ShapeDtypeStruct((sources * receivers, LAGS), jnp.bfloat16),
        in_specs=[vmem, smem, smem, vmem, pl.BlockSpec(memory_space=pl.ANY)],
        out_specs=pl.BlockSpec(memory_space=pl.ANY),
        scratch_shapes=[
            pltpu.VMEM(table.shape, table.dtype),
            pltpu.VMEM((groups, receivers, depth), jnp.bfloat16),
            pltpu.VMEM((n, receivers, depth), jnp.bfloat16),
            pltpu.VMEM((n, receivers, depth), jnp.bfloat16),
            pltpu.VMEM((groups, sources, depth), jnp.bfloat16),
            pltpu.VMEM((groups, receivers * 2 * GROUP, depth), jnp.bfloat16),
            pltpu.VMEM((receivers, 2, groups * GROUP, sources), jnp.bfloat16),
            pltpu.VMEM((LAGS // 128, sources * (receivers + 8), 128), jnp.float32),
            pltpu.VMEM((sources * receivers, LAGS), jnp.bfloat16),
            pltpu.VMEM((sources, 128), jnp.float32),
            pltpu.VMEM((n, 8, sources), jnp.float32),
            pltpu.VMEM((sources, 128), jnp.float32),
            dma((per, n)),
            dma((per, n)),
            dma((per, 4, n)),
            dma((per, n)),
            dma((n,)),
            dma((n,)),
            dma((chunks,)),
            dma(()),
        ],
        compiler_params=pltpu.CompilerParams(
            collective_id=0, has_side_effects=True, vmem_limit_bytes=VMEM_LIMIT
        ),
        name="fused",
    )(
        spectra.reshape(receivers * windows, width), blocks, valid,
        jnp.asarray(by_row), table,
    )


def correlate_kernel(s_ref, x_ref, table_ref, trace_ref, peak_ref, cross, pk):
    groups, rows, depth = s_ref.shape
    receivers = x_ref.shape[1]
    half = depth // 2
    diag = lax.rem(lax.broadcasted_iota(jnp.int32, (GROUP, depth), 1), GROUP) == (
        lax.broadcasted_iota(jnp.int32, (GROUP, depth), 0)
    )

    def first(g, carry):
        v = x_ref[g].astype(jnp.float32)
        turned = jnp.concatenate([v[:, half:], -v[:, :half]], axis=1)
        both = jnp.stack([v, turned], axis=1)
        spread = jnp.where(diag[None, None], both[:, :, None, :], 0.0).astype(jnp.bfloat16)
        spread = spread.reshape(receivers * 2 * GROUP, depth)
        out = lax.dot_general(
            spread, s_ref[g], (((1,), (1,)), ((), ())), preferred_element_type=jnp.float32
        ).astype(jnp.bfloat16)
        where = pl.ds(pl.multiple_of(g * GROUP, GROUP), GROUP)
        cross[:, :, where, :] = out.reshape(receivers, 2, GROUP, rows)
        return carry

    lax.fori_loop(0, groups, first, 0)

    pk[...] = jnp.zeros_like(pk)
    step = 4
    lanes = pk.shape[1]

    def second(i, carry):
        parts = [
            cross[i * step + q].reshape(2 * groups * GROUP, rows).T for q in range(step)
        ]
        out = jnp.dot(
            jnp.concatenate(parts, axis=0), table_ref[...], preferred_element_type=jnp.float32
        )
        best = pk[...]
        for q in range(step):
            piece = out[q * rows:(q + 1) * rows]
            for c in range(LAGS // lanes):
                cols = piece[:, c * lanes:(c + 1) * lanes]
                trace_ref[c, pl.ds(i * step + q, rows, stride=receivers), :] = cols
                best = jnp.maximum(best, jnp.abs(cols))
        pk[...] = best
        return carry

    lax.fori_loop(0, receivers // step, second, 0)
    peak_ref[...] = jnp.broadcast_to(jnp.max(pk[...].T, axis=0, keepdims=True), peak_ref.shape)


def correlate(sources, x, table):
    groups, rows, depth = sources.shape
    receivers = x.shape[1]
    vmem = pl.BlockSpec(memory_space=pltpu.VMEM)
    return pl.pallas_call(
        correlate_kernel,
        out_shape=(
            jax.ShapeDtypeStruct((LAGS // 128, rows * receivers, 128), jnp.float32),
            jax.ShapeDtypeStruct((8, rows), jnp.float32),
        ),
        in_specs=[vmem] * 3,
        out_specs=(vmem, vmem),
        scratch_shapes=[
            pltpu.VMEM((receivers, 2, groups * GROUP, rows), jnp.bfloat16),
            pltpu.VMEM((rows, 128), jnp.float32),
        ],
        compiler_params=pltpu.CompilerParams(vmem_limit_bytes=VMEM_LIMIT),
        name="correlate",
    )(sources, x, table)


def scale_kernel(block, receivers, peak_ref, trace_ref, out_ref):
    i = pl.program_id(0)
    for q in range(block):
        peak = jnp.full((1, 128), peak_ref[0, i * block + q], jnp.float32)
        inverse = 1.0 / (peak + 1e-06)
        here = slice(q * receivers, (q + 1) * receivers)
        for c in range(LAGS // 128):
            cols = slice(c * 128, (c + 1) * 128)
            out_ref[here, cols] = (trace_ref[c, here, :] * inverse).astype(jnp.bfloat16)


def scale(trace, peak, receivers):
    block = 16
    total = trace.shape[1]
    steps = total // (block * receivers)
    return pl.pallas_call(
        functools.partial(scale_kernel, block, receivers),
        out_shape=jax.ShapeDtypeStruct((total, LAGS), jnp.bfloat16),
        grid=(steps,),
        in_specs=[
            pl.BlockSpec(memory_space=pltpu.SMEM),
            pl.BlockSpec((LAGS // 128, block * receivers, 128), lambda i: (0, i, 0)),
        ],
        out_specs=pl.BlockSpec((block * receivers, LAGS), lambda i: (i, 0)),
        compiler_params=pltpu.CompilerParams(vmem_limit_bytes=VMEM_LIMIT),
        name="scale",
    )(peak, trace)


def shards(n, spectra, source_blocks, window_valid):
    receivers, windows, width = spectra.shape
    bins = width // 2
    groups = bins // GROUP
    num_steps = source_blocks.shape[0]
    table = jnp.asarray(build_table(bins, LAGS))
    if n == 16:
        out = fused(n, spectra, source_blocks, window_valid, table)
    else:
        x = spectra.reshape(receivers, windows, 2, groups, GROUP).transpose(3, 0, 2, 1, 4)
        x = x.reshape(groups, receivers, 2 * windows * GROUP)
        mask = jnp.tile(jnp.repeat(window_valid.astype(jnp.bfloat16), GROUP), 2)[None, :]
        roots = source_blocks.reshape(-1) // (receivers // SOURCE)
        mine = (roots == lax.axis_index("chan"))[None, :, None, None]
        picked = jnp.where(mine, (x * mask)[:, None], jnp.zeros((), x.dtype))
        sources = lax.psum(picked.reshape(groups, -1, x.shape[2]), "chan")
        trace, peak = correlate(sources, x, table)
        out = scale(trace, lax.pmax(peak, "chan"), receivers)
    return out.reshape(num_steps, 2, SOURCE, receivers, LAGS)


def solution(mesh):
    placed = (P(("parts", "chan"), None, None), P("parts", None), P("parts"))
    return jax.shard_map(
        functools.partial(shards, mesh.shape["chan"]),
        mesh=mesh,
        in_specs=placed,
        out_specs=P(None, None, None, ("parts", "chan"), None),
        check_vma=False,
    )
```
